32 devices in a mesh: dp: 8 (over z, y), mp: 4 (over x, core).
Axes of the slice: x: 2, y: 2, z: 4, core: 2. Of those that a mesh axis runs over, the one named last changes fastest.
Arguments:
- samples: bfloat16 [6144, 8192], P('dp', 'mp'), may hold values from -6 to 6
- gain: float32 [8192], P('mp'), may hold values from 0.1 to 1.9
- left_blocks: bfloat16 [64, 128, 128], P('mp'), may hold values from -0.5 to 0.5
- gate_blocks: bfloat16 [64, 128, 128], P('mp'), may hold values from -0.5 to 0.5
- right_blocks: bfloat16 [64, 128, 128], P('mp'), may hold values from -0.5 to 0.5
- cotangent: bfloat16 [6144, 8192], P('dp', 'mp'), may hold values from -6 to 6
Outputs:
- grad_input: bfloat16 [6144, 8192], P('dp', 'mp')
- grad_left: float32 [64, 128, 128], P('mp')
- grad_gate: float32 [64, 128, 128], P('mp')
- grad_right: float32 [64, 128, 128], P('mp')
The draws below stay inside these ranges and needn't reach their ends.
All inputs are finite; a program needn't handle non-finite values.
Results may differ from the reference program's by a relative error of at most 0.007.
Values may be sent and summed in bfloat16 or wider, within the bound.
A program may use at most 128 MiB of HBM per device.

```python
import jax
import jax.numpy as jnp
from jax import lax

W = 8192
BLOCK = 128
NBLK = 64
ROWS_DEV = 768
TOKENS = 6144


def block_levels(own_key, shape, split, least, largest):
    level, own = 1.0, jax.random.fold_in(own_key, 6)
    for position, shards_of in split:
        heights = jnp.exp(jax.random.uniform(jax.random.fold_in(own, position), (shards_of,), jnp.float32, least / len(split), largest / len(split)))
        level = level * jnp.repeat(heights, shape[position] // shards_of).reshape([-1 if axis == position else 1 for axis in range(len(shape))])
    return level


def gaussian(rng, extent, spread, reach, pieces=(), held_as=jnp.bfloat16):
    loudness = block_levels(rng, extent, pieces, -0.22, 0.18) if pieces else 1.0
    drawn = jax.random.normal(rng, extent, jnp.float32) * spread * loudness
    return jnp.minimum(jnp.maximum(drawn, -reach), reach).astype(held_as)


def setup_inputs(seed: int = 0) -> dict:
    seeds = jax.random.split(jax.random.key(seed), 7)
    samples = gaussian(seeds[0], (TOKENS, W), 1.0, 6.0, ((0, 8), (1, 4)))
    gain = jnp.clip(1.0 + 0.18 * jax.random.normal(seeds[1], (W,), jnp.float32), 0.1, 1.9)
    left_blocks = gaussian(seeds[2], (NBLK, BLOCK, BLOCK), BLOCK ** -0.5, 0.5, ((0, 4),))
    gate_blocks = gaussian(seeds[3], (NBLK, BLOCK, BLOCK), BLOCK ** -0.5, 0.5, ((0, 4),))
    right_blocks = gaussian(seeds[4], (NBLK, BLOCK, BLOCK), BLOCK ** -0.5, 0.5, ((0, 4),))
    cotangent = gaussian(seeds[5], (TOKENS, W), 1.0, 6.0, ((0, 8), (1, 4)))
    return {"samples": samples, "gain": gain, "left_blocks": left_blocks, "gate_blocks": gate_blocks, "right_blocks": right_blocks, "cotangent": cotangent}


def frame_block(xblk, dyblk, gain, left_blocks, gate_blocks, right_blocks):
    count = xblk.shape[0]
    xf = xblk.astype(jnp.float32)
    rstd = lax.rsqrt(lax.optimization_barrier(jnp.sum(xf * xf, axis=1, keepdims=True)) / W + 1e-05)
    xn = (xf * rstd * gain).astype(jnp.bfloat16).reshape(count, NBLK, BLOCK).astype(jnp.float32)
    lf = left_blocks.astype(jnp.float32)
    gf = gate_blocks.astype(jnp.float32)
    rf = right_blocks.astype(jnp.float32)
    a = jnp.einsum('tic,icj->tij', xn, lf)
    g = jnp.einsum('tic,icj->tij', xn, gf)
    sg = jax.nn.silu(g)
    h = (a * sg).astype(jnp.bfloat16)
    p = h.reshape(count, NBLK, NBLK, 2).transpose(0, 2, 1, 3).reshape(count, NBLK, BLOCK).astype(jnp.float32)
    dyr = dyblk.reshape(count, NBLK, BLOCK).astype(jnp.float32)
    d_right = jnp.einsum('tkc,tkm->kcm', p, dyr)
    dp = jnp.einsum('tkm,kcm->tkc', dyr, rf).astype(jnp.bfloat16)
    dh = dp.reshape(count, NBLK, NBLK, 2).transpose(0, 2, 1, 3).reshape(count, NBLK, BLOCK).astype(jnp.float32)
    sig = jax.nn.sigmoid(g)
    da = (dh * sg).astype(jnp.bfloat16).astype(jnp.float32)
    dg = (dh * a * sig * (1.0 + g * (1.0 - sig))).astype(jnp.bfloat16).astype(jnp.float32)
    d_left = jnp.einsum('tic,tij->icj', xn, da)
    d_gate = jnp.einsum('tic,tij->icj', xn, dg)
    dxn = jnp.einsum('tij,icj->tic', da, lf) + jnp.einsum('tij,icj->tic', dg, gf)
    q = dxn.reshape(count, W) * gain
    mu = lax.optimization_barrier(jnp.sum(q * xf, axis=1, keepdims=True)) / W
    dx = (dyblk.astype(jnp.float32) + rstd * (q - xf * rstd * rstd * mu)).astype(jnp.bfloat16)
    return (dx, d_left, d_gate, d_right)

def reference(samples, gain, left_blocks, gate_blocks, right_blocks, cotangent):
    nsteps = TOKENS // ROWS_DEV
    xs = samples.reshape(nsteps, ROWS_DEV, W)
    dys = cotangent.reshape(nsteps, ROWS_DEV, W)
    zero = jnp.zeros((NBLK, BLOCK, BLOCK), jnp.float32)

    def step(carry, inputs):
        dx, d_left, d_gate, d_right = frame_block(inputs[0], inputs[1], gain, left_blocks, gate_blocks, right_blocks)
        return ((carry[0] + d_left, carry[1] + d_gate, carry[2] + d_right), dx)
    sums, dxs = lax.scan(step, (zero, zero, zero), (xs, dys))
    return (dxs.reshape(TOKENS, W), sums[0], sums[1], sums[2])
```

```python
import functools

import jax
import jax.numpy as jnp
from jax import lax
from jax.experimental import pallas as pl
from jax.experimental.pallas import tpu as pltpu
from jax.sharding import PartitionSpec as P

F32 = jnp.float32
BF16 = jnp.bfloat16
MESH = pl.DeviceIdType.MESH


def nn(x, y):
    return lax.dot_general(x, y, (((1,), (0,)), ((), ())), preferred_element_type=F32)


def nt(x, y):
    return lax.dot_general(x, y, (((1,), (1,)), ((), ())), preferred_element_type=F32)


def tn(x, y):
    return lax.dot_general(x, y, (((0,), (0,)), ((), ())), preferred_element_type=F32)


def kernel(
    ndp, nmp, width, units,
    x_hbm, gain_ref, left_hbm, gate_hbm, right_hbm, cot_hbm,
    out_hbm, sums_hbm,
    x, cot, left, gate, right, dpt, d, hs, y, p, xnt, at, gt, qs,
    grads, arrived, total, rstd, ssx, mux,
    in_sem, wt_sem, out_sem, loc_sem,
    ss_s, ss_r, dp_s, dp_r, h_s, h_r, mu_s, mu_r, rs_s, rs_r, ag_s, ag_r,
):
    nl, rows, blk = x.shape
    me_d, me = lax.axis_index("dp"), lax.axis_index("mp")
    groups = nl // 8

    def cols(ref, i):
        return ref.at[:, pl.ds(pl.multiple_of(i * blk, blk), blk)]

    def fetch_x(i):
        return pltpu.make_async_copy(cols(x_hbm, i), x.at[i], in_sem.at[0, i])

    def fetch_cot(i):
        return pltpu.make_async_copy(cols(cot_hbm, i), cot.at[i], in_sem.at[1, i])

    def loop(n, f):
        def step(i, carry):
            f(i)
            return carry
        lax.fori_loop(0, n, step, 0)

    loop(nl, lambda i: fetch_x(i).start())
    weights = [
        pltpu.make_async_copy(src, dst, wt_sem.at[w])
        for w, (src, dst) in enumerate(((right_hbm, right), (left_hbm, left), (gate_hbm, gate)))
    ]
    weights[0].start()
    loop(nl, lambda i: fetch_cot(i).start())
    weights[1].start()
    weights[2].start()

    def peer_mp(o):
        return (me_d, lax.rem(me + o, nmp))

    def peer_dp(o):
        return (lax.rem(me_d + o, ndp), me)

    barrier = pltpu.get_barrier_semaphore()
    for o in range(1, nmp):
        pl.semaphore_signal(barrier, inc=1, device_id=peer_mp(o), device_id_type=MESH)
    loop(ndp - 1, lambda o: pl.semaphore_signal(
        barrier, inc=1, device_id=peer_dp(o + 1), device_id_type=MESH))

    def remote(src, dst, s, r, dev):
        return pltpu.make_async_remote_copy(
            src_ref=src, dst_ref=dst, send_sem=s, recv_sem=r, device_id=dev, device_id_type=MESH)

    def add_square(i, acc):
        fetch_x(i).wait()
        v = x[i].astype(F32)
        return acc + v * v
    acc = lax.fori_loop(0, nl, add_square, jnp.zeros((rows, blk), F32))
    ssx[0] = jnp.broadcast_to(jnp.sum(acc.T, axis=0, keepdims=True), (8, rows))
    pl.semaphore_wait(barrier, nmp - 1 + ndp - 1)

    def ss_copy(o):
        return remote(ssx.at[0], ssx.at[o], ss_s.at[o], ss_r.at[o], peer_mp(o))
    for o in range(1, nmp):
        ss_copy(o).start()

    weights[0].wait()

    def back_right(k):
        fetch_cot(k).wait()
        dpt[k] = nt(right[k], cot[k]).astype(BF16)
    loop(nl, back_right)

    def dp_copy(o, g):
        dest = lax.rem(me + o, nmp)
        return remote(
            dpt.at[:, pl.ds(pl.multiple_of(16 * (groups * dest + g), 16), 16)],
            d.at[g, pl.ds(nl * me, nl)],
            dp_s.at[o, g], dp_r.at[o, g], peer_mp(o))

    def dp_local(g):
        return pltpu.make_async_copy(
            dpt.at[:, pl.ds(pl.multiple_of(16 * (groups * me + g), 16), 16)],
            d.at[g, pl.ds(nl * me, nl)], loc_sem.at[0, g])
    for g in range(groups):
        for o in range(1, nmp):
            dp_copy(o, g).start()
        dp_local(g).start()

    r = lax.broadcasted_iota(jnp.int32, (128, 128), 0)
    c = lax.broadcasted_iota(jnp.int32, (128, 128), 1)
    moved = ((c & 14) << 3) | ((c >> 4) << 1) | (c & 1)
    swap = jnp.where(r == moved, 1.0, 0.0).astype(BF16)

    for o in range(1, nmp):
        ss_copy(o).wait()
    squares = ssx[0, 0:1]
    for o in range(1, nmp):
        squares = squares + ssx[o, 0:1]
    inv_row = lax.rsqrt(squares / width + 1e-05)
    rstd[...] = jnp.broadcast_to(inv_row, (blk, rows)).T
    weights[1].wait()
    weights[2].wait()

    def forward(i):
        xn = (x[i].astype(F32) * rstd[...] * gain_ref[i]).astype(BF16)
        t = xn.T
        xnt[i] = t
        a = tn(left[i], t)
        v = tn(gate[i], t)
        at[i] = a
        gt[i] = v
        hs[i] = (a * (v / (1.0 + jnp.exp(-v)))).astype(BF16)
    loop(nl, forward)

    nk = y.shape[1]
    for g in range(groups):
        def permute(kk):
            rows16 = pl.ds(pl.multiple_of(16 * kk, 16), 16)
            block = hs[8 * g:8 * g + 8, rows16, :].reshape(128, rows)
            y[g, pl.ds(8 * kk, 8)] = nn(swap, block).astype(BF16).reshape(8, 16, rows)
        loop(nk // 8, permute)

    halves = nl // 8

    def h_copy(o, g, half):
        dest = lax.rem(me + o, nmp)
        return remote(
            y.at[g, pl.ds(nl * dest + 8 * half, 8)],
            p.at[pl.ds(8 * half, 8), pl.ds(pl.multiple_of(16 * (groups * me + g), 16), 16)],
            h_s.at[o, g, half], h_r.at[o, g, half], peer_mp(o))

    def h_local(g, half):
        return pltpu.make_async_copy(
            y.at[g, pl.ds(nl * me + 8 * half, 8)],
            p.at[pl.ds(8 * half, 8), pl.ds(pl.multiple_of(16 * (groups * me + g), 16), 16)],
            loc_sem.at[1 + half, g])
    for half in range(halves):
        for g in range(groups):
            for o in range(1, nmp):
                h_copy(o, g, half).start()
            h_local(g, half).start()

    def rs_copy(u, o):
        off, n = units[u]
        size = n // ndp
        dest = lax.rem(me_d + o, ndp)
        return remote(
            grads.at[pl.ds(pl.multiple_of(off + dest * size, 16), size)],
            arrived.at[o, pl.ds(off // ndp, size)],
            rs_s.at[u, o], rs_r.at[u, o], peer_dp(o))

    def ag_copy(u, o):
        off, n = units[u]
        size = n // ndp
        own = pl.ds(pl.multiple_of(off + me_d * size, 16), size)
        return remote(total.at[own], total.at[own], ag_s.at[u, o], ag_r.at[u, o], peer_dp(o))

    def scatter(u):
        loop(ndp - 1, lambda o: rs_copy(u, o + 1).start())

    def gather(u):
        off, n = units[u]
        size = n // ndp
        own = pl.ds(pl.multiple_of(off + me_d * size, 16), size)

        def add(o, acc):
            rs_copy(u, o + 1).wait()
            return acc + arrived[o + 1, pl.ds(off // ndp, size)].astype(F32)
        acc = lax.fori_loop(0, ndp - 1, add, grads[own].astype(F32))
        total[own] = acc.astype(BF16)
        loop(ndp - 1, lambda o: ag_copy(u, o + 1).start())

    mux[0] = jnp.zeros((8, rows), F32)
    for g in range(groups):
        for o in range(1, nmp):
            dp_copy(o, g).wait()
        dp_local(g).wait()

        def unpermute(kk):
            block = d[g, pl.ds(8 * kk, 8)].reshape(128, rows)
            rows16 = pl.ds(pl.multiple_of(16 * kk, 16), 16)
            hs[8 * g:8 * g + 8, rows16, :] = nn(swap, block).astype(BF16).reshape(8, 16, rows)
        loop(nk // 8, unpermute)

        def backward(j):
            i = 8 * g + j
            dh = hs[i].astype(F32)
            v = gt[i]
            s = 1.0 / (1.0 + jnp.exp(-v))
            da = (dh * (v * s)).astype(BF16)
            dg = (dh * at[i] * s * (1.0 + v * (1.0 - s))).astype(BF16)
            t = xnt[i]
            base = units[g][0]
            grads[pl.ds(pl.multiple_of(base + j * blk, 16), blk)] = nt(t, da).astype(BF16)
            grads[pl.ds(pl.multiple_of(base + (8 + j) * blk, 16), blk)] = nt(t, dg).astype(BF16)
            dxn = nn(left[i], da) + nn(gate[i], dg)
            mux[0] = mux[0] + jnp.sum((dxn * t.astype(F32)).reshape(blk // 8, 8, rows), axis=0)
            qs[i] = cot[i].astype(F32) + rstd[...] * (dxn.T * gain_ref[i])
        loop(8, backward)
        scatter(g)

    def mu_copy(o):
        return remote(mux.at[0], mux.at[o], mu_s.at[o], mu_r.at[o], peer_mp(o))
    for o in range(1, nmp):
        mu_copy(o).start()

    for g in range(groups):
        gather(g)

    for half in range(halves):
        for g in range(groups):
            for o in range(1, nmp):
                h_copy(o, g, half).wait()
            h_local(g, half).wait()
        u = groups + half

        def right_grad(j):
            k = 8 * half + j
            grads[pl.ds(pl.multiple_of(units[u][0] + j * blk, 16), blk)] = nn(p[k], cot[k]).astype(BF16)
        loop(8, right_grad)
        scatter(u)

    for o in range(1, nmp):
        mu_copy(o).wait()
    inner = mux[0]
    for o in range(1, nmp):
        inner = inner + mux[o]
    square = inv_row * inv_row
    factor = jnp.sum(inner, axis=0, keepdims=True) * square / width
    qs_factor = jnp.broadcast_to(factor, (blk, rows)).T

    def store_out(i):
        return pltpu.make_async_copy(x.at[i], cols(out_hbm, i), out_sem.at[i])

    def finish(i):
        x[i] = (qs[i] - x[i].astype(F32) * qs_factor).astype(BF16)
        store_out(i).start()
    loop(nl, finish)

    for half in range(halves):
        gather(groups + half)
    for u in range(len(units)):
        def settle(o):
            ag_copy(u, o + 1).wait()
        loop(ndp - 1, settle)
    sums = pltpu.make_async_copy(total, sums_hbm, wt_sem.at[0])
    sums.start()
    loop(nl, lambda i: store_out(i).wait())
    sums.wait()


def body(samples, gain, left_blocks, gate_blocks, right_blocks, cotangent, *, ndp, nmp):
    rows, width_local = samples.shape
    nl, blk = left_blocks.shape[0], left_blocks.shape[1]
    groups = nl // 8
    nk = nl * nmp
    units = [(g * 16 * blk, 16 * blk) for g in range(groups)]
    units += [(2 * nl * blk + 8 * blk * v, 8 * blk) for v in range(groups)]
    flat = 3 * nl * blk
    dma = pltpu.SemaphoreType.DMA
    any_space = pl.BlockSpec(memory_space=pl.ANY)
    grad_input, sums = pl.pallas_call(
        functools.partial(kernel, ndp, nmp, float(width_local * nmp), units),
        out_shape=(
            jax.ShapeDtypeStruct((rows, width_local), BF16),
            jax.ShapeDtypeStruct((flat, blk), BF16),
        ),
        in_specs=[any_space, pl.BlockSpec(memory_space=pltpu.VMEM)] + [any_space] * 4,
        out_specs=(any_space, any_space),
        scratch_shapes=[
            pltpu.VMEM((nl, rows, blk), BF16),
            pltpu.VMEM((nl, rows, blk), BF16),
            pltpu.VMEM((nl, blk, blk), BF16),
            pltpu.VMEM((nl, blk, blk), BF16),
            pltpu.VMEM((nl, blk, blk), BF16),
            pltpu.VMEM((nl, blk, rows), BF16),
            pltpu.VMEM((groups, nk, 16, rows), BF16),
            pltpu.VMEM((nl, blk, rows), BF16),
            pltpu.VMEM((groups, nk, 16, rows), BF16),
            pltpu.VMEM((nl, blk, rows), BF16),
            pltpu.VMEM((nl, blk, rows), BF16),
            pltpu.VMEM((nl, blk, rows), F32),
            pltpu.VMEM((nl, blk, rows), F32),
            pltpu.VMEM((nl, rows, blk), F32),
            pltpu.VMEM((flat, blk), BF16),
            pltpu.VMEM((ndp, flat // ndp, blk), BF16),
            pltpu.VMEM((flat, blk), BF16),
            pltpu.VMEM((rows, blk), F32),
            pltpu.VMEM((nmp, 8, rows), F32),
            pltpu.VMEM((nmp, 8, rows), F32),
            dma((2, nl)), dma((3,)), dma((nl,)), dma((1 + groups, groups)),
            dma((nmp,)), dma((nmp,)),
            dma((nmp, groups)), dma((nmp, groups)),
            dma((nmp, groups, groups)), dma((nmp, groups, groups)),
            dma((nmp,)), dma((nmp,)),
            dma((2 * groups, ndp)), dma((2 * groups, ndp)),
            dma((2 * groups, ndp)), dma((2 * groups, ndp)),
        ],
        compiler_params=pltpu.CompilerParams(
            collective_id=0, has_side_effects=True, vmem_limit_bytes=60 * 1024 * 1024),
    )(samples, gain.reshape(nl, 1, blk), left_blocks, gate_blocks, right_blocks, cotangent)
    head = sums[:2 * nl * blk].reshape(groups, 2, 8, blk, blk)
    grad_left = head[:, 0].reshape(nl, blk, blk).astype(F32)
    grad_gate = head[:, 1].reshape(nl, blk, blk).astype(F32)
    grad_right = sums[2 * nl * blk:].reshape(nl, blk, blk).astype(F32)
    return grad_input, grad_left, grad_gate, grad_right


def solution(mesh):
    blocks = P("mp", None, None)
    return jax.shard_map(
        functools.partial(body, ndp=mesh.shape["dp"], nmp=mesh.shape["mp"]),
        mesh=mesh,
        in_specs=(P("dp", "mp"), P("mp"), blocks, blocks, blocks, P("dp", "mp")),
        out_specs=(P("dp", "mp"), blocks, blocks, blocks),
        check_vma=False,
    )
```

```python
import functools

import jax
import jax.numpy as jnp
from jax import lax
from jax.experimental import pallas as pl
from jax.experimental.pallas import tpu as pltpu
from jax.sharding import PartitionSpec as P

F32 = jnp.float32
BF16 = jnp.bfloat16
MESH = pl.DeviceIdType.MESH


def nn(x, y):
    return lax.dot_general(x, y, (((1,), (0,)), ((), ())), preferred_element_type=F32)


def nt(x, y):
    return lax.dot_general(x, y, (((1,), (1,)), ((), ())), preferred_element_type=F32)


def tn(x, y):
    return lax.dot_general(x, y, (((0,), (0,)), ((), ())), preferred_element_type=F32)


def kernel(
    ndp, nmp, width, units, direct,
    x_hbm, gain_ref, left_hbm, gate_hbm, right_hbm, cot_hbm,
    out_hbm, left_out, gate_out, right_out,
    x, cot, left, gate, right, dpt, d, hs, y, p, xnt, at, gt, qs,
    grads, arrived, total, rstd, ssx, mux,
    in_sem, wt_sem, out_sem, loc_sem, res_sem,
    ss_s, ss_r, dp_s, dp_r, h_s, h_r, mu_s, mu_r, rs_s, rs_r, ag_s, ag_r,
):
    nl, rows, blk = x.shape
    me_d, me = lax.axis_index("dp"), lax.axis_index("mp")
    groups = nl // 8

    def cols(ref, i):
        return ref.at[:, pl.ds(pl.multiple_of(i * blk, blk), blk)]

    def fetch_x(i):
        return pltpu.make_async_copy(cols(x_hbm, i), x.at[i], in_sem.at[0, i])

    def fetch_cot(i):
        return pltpu.make_async_copy(cols(cot_hbm, i), cot.at[i], in_sem.at[1, i])

    def loop(n, f):
        def step(i, carry):
            f(i)
            return carry
        lax.fori_loop(0, n, step, 0)

    weights = [
        pltpu.make_async_copy(src, dst, wt_sem.at[w])
        for w, (src, dst) in enumerate(((right_hbm, right), (left_hbm, left), (gate_hbm, gate)))
    ]
    weights[0].start()
    loop(nl, lambda i: fetch_cot(i).start())
    loop(nl, lambda i: fetch_x(i).start())
    weights[1].start()
    weights[2].start()

    def peer_mp(o):
        return (me_d, lax.rem(me + o, nmp))

    def peer_dp(o):
        return (lax.rem(me_d + o, ndp), me)

    barrier = pltpu.get_barrier_semaphore()
    for o in range(1, nmp):
        pl.semaphore_signal(barrier, inc=1, device_id=peer_mp(o), device_id_type=MESH)
    loop(ndp - 1, lambda o: pl.semaphore_signal(
        barrier, inc=1, device_id=peer_dp(o + 1), device_id_type=MESH))

    def remote(src, dst, s, r, dev):
        return pltpu.make_async_remote_copy(
            src_ref=src, dst_ref=dst, send_sem=s, recv_sem=r, device_id=dev, device_id_type=MESH)

    weights[0].wait()

    def back_right(k):
        fetch_cot(k).wait()
        dpt[k] = nt(right[k], cot[k]).astype(BF16)
    loop(nl, back_right)

    def dp_copy(o, g):
        dest = lax.rem(me + o, nmp)
        return remote(
            dpt.at[:, pl.ds(pl.multiple_of(16 * (groups * dest + g), 16), 16)],
            d.at[g, pl.ds(nl * me, nl)],
            dp_s.at[o, g], dp_r.at[o, g], peer_mp(o))

    def dp_local(g):
        return pltpu.make_async_copy(
            dpt.at[:, pl.ds(pl.multiple_of(16 * (groups * me + g), 16), 16)],
            d.at[g, pl.ds(nl * me, nl)], loc_sem.at[0, g])
    def send_dp(g):
        for o in range(1, nmp):
            dp_copy(o, g).start()
        dp_local(g).start()
    pl.semaphore_wait(barrier, nmp - 1 + ndp - 1)
    send_dp(0)

    def add_square(i, acc):
        fetch_x(i).wait()
        v = x[i].astype(F32)
        return acc + v * v
    acc = lax.fori_loop(0, nl, add_square, jnp.zeros((rows, blk), F32))
    ssx[0] = jnp.broadcast_to(jnp.sum(acc.T, axis=0, keepdims=True), (8, rows))

    def ss_copy(o):
        return remote(ssx.at[0], ssx.at[o], ss_s.at[o], ss_r.at[o], peer_mp(o))
    for o in range(1, nmp):
        ss_copy(o).start()

    for g in range(1, groups):
        send_dp(g)

    r = lax.broadcasted_iota(jnp.int32, (128, 128), 0)
    c = lax.broadcasted_iota(jnp.int32, (128, 128), 1)
    moved = ((c & 14) << 3) | ((c >> 4) << 1) | (c & 1)
    swap = jnp.where(r == moved, 1.0, 0.0).astype(BF16)

    for o in range(1, nmp):
        ss_copy(o).wait()
    squares = ssx[0, 0:1]
    for o in range(1, nmp):
        squares = squares + ssx[o, 0:1]
    inv_row = lax.rsqrt(squares / width + 1e-05)
    rstd[...] = jnp.broadcast_to(inv_row, (blk, rows)).T
    weights[1].wait()
    weights[2].wait()

    def forward(i):
        xn = (x[i].astype(F32) * rstd[...] * gain_ref[i]).astype(BF16)
        t = xn.T
        xnt[i] = t
        a = tn(left[i], t)
        v = tn(gate[i], t)
        at[i] = a
        gt[i] = v
        hs[i] = (a * (v / (1.0 + jnp.exp(-v)))).astype(BF16)
    loop(nl, forward)

    nk = y.shape[1]
    for g in range(groups):
        def permute(kk):
            rows16 = pl.ds(pl.multiple_of(16 * kk, 16), 16)
            block = hs[8 * g:8 * g + 8, rows16, :].reshape(128, rows)
            y[g, pl.ds(8 * kk, 8)] = nn(swap, block).astype(BF16).reshape(8, 16, rows)
        loop(nk // 8, permute)

    parts = len(units) - groups
    span = nl // parts

    def h_copy(o, g, part):
        dest = lax.rem(me + o, nmp)
        return remote(
            y.at[g, pl.ds(nl * dest + span * part, span)],
            p.at[pl.ds(span * part, span), pl.ds(pl.multiple_of(16 * (groups * me + g), 16), 16)],
            h_s.at[o, g, part], h_r.at[o, g, part], peer_mp(o))

    def h_local(g, part):
        return pltpu.make_async_copy(
            y.at[g, pl.ds(nl * me + span * part, span)],
            p.at[pl.ds(span * part, span), pl.ds(pl.multiple_of(16 * (groups * me + g), 16), 16)],
            loc_sem.at[1 + part, g])

    def send_h(part):
        for g in range(groups):
            for o in range(1, nmp):
                h_copy(o, g, part).start()
            h_local(g, part).start()
    for part in range(parts // 2):
        send_h(part)

    bits = [1 << v for v in range(ndp.bit_length() - 1)]

    def chunk(start, size):
        return pl.ds(pl.multiple_of(start, 16), size)

    def halving(u):
        off, n = units[u]
        stages, lo = [], off
        for v, bit in enumerate(bits):
            size = n >> (v + 1)
            mine = lax.rem(me_d // bit, 2)
            keep, give = lo + mine * size, lo + (1 - mine) * size
            stages.append((v, size, keep, give, (me_d + bit * (1 - 2 * mine), me)))
            lo = keep
        for v, size, keep, give, dev in stages:
            slot = chunk(off + n - 2 * size, size)
            copy = remote(grads.at[chunk(give, size)], arrived.at[slot], rs_s.at[u, v], rs_r.at[u, v], dev)
            copy.start()
            yield
            copy.wait()
            value = (grads[chunk(keep, size)].astype(F32) + arrived[slot].astype(F32)).astype(BF16)
            if v + 1 < len(stages):
                grads[chunk(keep, size)] = value
            else:
                total[chunk(keep, size)] = value
        for v, size, keep, give, dev in reversed(stages):
            held = total.at[chunk(keep, size)]
            copy = remote(held, held, ag_s.at[u, v], ag_r.at[u, v], dev)
            copy.start()
            yield
            copy.wait()

    def straight(u):
        off, n = units[u]
        size = n // ndp
        own = chunk(off + me_d * size, size)

        def rs_copy(o):
            dest = lax.rem(me_d + o, ndp)
            return remote(
                grads.at[chunk(off + dest * size, size)], arrived.at[chunk(off + o * size, size)],
                rs_s.at[u, o], rs_r.at[u, o], peer_dp(o))

        def ag_copy(o):
            return remote(total.at[own], total.at[own], ag_s.at[u, o], ag_r.at[u, o], peer_dp(o))
        loop(ndp - 1, lambda o: rs_copy(o + 1).start())
        yield

        def add(o, acc):
            rs_copy(o + 1).wait()
            return acc + arrived[chunk(off + (o + 1) * size, size)].astype(F32)
        total[own] = lax.fori_loop(0, ndp - 1, add, grads[own].astype(F32)).astype(BF16)
        loop(ndp - 1, lambda o: ag_copy(o + 1).start())
        yield
        loop(ndp - 1, lambda o: ag_copy(o + 1).wait())

    def result_copies(u):
        off, n = units[u]
        if u < groups:
            place = pl.ds(u * n // 2, n // 2)
            return [
                pltpu.make_async_copy(total.at[pl.ds(off, n // 2)], left_out.at[place], res_sem.at[u, 0]),
                pltpu.make_async_copy(total.at[pl.ds(off + n // 2, n // 2)], gate_out.at[place], res_sem.at[u, 1]),
            ]
        return [pltpu.make_async_copy(
            total.at[pl.ds(off, n)], right_out.at[pl.ds((u - groups) * n, n)], res_sem.at[u, 0])]

    running = {}

    def tick(u):
        if u not in running:
            running[u] = straight(u) if u >= len(units) - direct else halving(u)
        try:
            next(running[u])
            return True
        except StopIteration:
            return False

    finished = set()

    def advance():
        for u in sorted(running):
            if u not in finished and not tick(u):
                finished.add(u)
                for copy in result_copies(u):
                    copy.start()

    mux[0] = jnp.zeros((8, rows), F32)
    for g in range(groups):
        for o in range(1, nmp):
            dp_copy(o, g).wait()
        dp_local(g).wait()

        def unpermute(kk):
            block = d[g, pl.ds(8 * kk, 8)].reshape(128, rows)
            rows16 = pl.ds(pl.multiple_of(16 * kk, 16), 16)
            hs[8 * g:8 * g + 8, rows16, :] = nn(swap, block).astype(BF16).reshape(8, 16, rows)
        loop(nk // 8, unpermute)

        def backward(j):
            i = 8 * g + j
            dh = hs[i].astype(F32)
            v = gt[i]
            s = 1.0 / (1.0 + jnp.exp(-v))
            da = (dh * (v * s)).astype(BF16)
            dg = (dh * at[i] * s * (1.0 + v * (1.0 - s))).astype(BF16)
            t = xnt[i]
            base = units[g][0]
            grads[pl.ds(pl.multiple_of(base + j * blk, 16), blk)] = nt(t, da).astype(BF16)
            grads[pl.ds(pl.multiple_of(base + (8 + j) * blk, 16), blk)] = nt(t, dg).astype(BF16)
            dxn = nn(left[i], da) + nn(gate[i], dg)
            mux[0] = mux[0] + jnp.sum((dxn * t.astype(F32)).reshape(blk // 8, 8, rows), axis=0)
            qs[i] = cot[i].astype(F32) + rstd[...] * (dxn.T * gain_ref[i])
        loop(8, backward)
        tick(g)
        if g + 1 < groups:
            advance()

    def mu_copy(o):
        return remote(mux.at[0], mux.at[o], mu_s.at[o], mu_r.at[o], peer_mp(o))
    for o in range(1, nmp):
        mu_copy(o).start()

    for part in range(parts // 2, parts):
        send_h(part)
    advance()
    advance()

    def store_out(i):
        return pltpu.make_async_copy(x.at[i], cols(out_hbm, i), out_sem.at[i])

    def finish_input():
        for o in range(1, nmp):
            mu_copy(o).wait()
        inner = mux[0]
        for o in range(1, nmp):
            inner = inner + mux[o]
        factor = jnp.sum(inner, axis=0, keepdims=True) * (inv_row * inv_row) / width
        factors = jnp.broadcast_to(factor, (blk, rows)).T

        def finish(i):
            x[i] = (qs[i] - x[i].astype(F32) * factors).astype(BF16)
            store_out(i).start()
        loop(nl, finish)

    for part in range(parts):
        if part == parts - 1:
            finish_input()
        for g in range(groups):
            for o in range(1, nmp):
                h_copy(o, g, part).wait()
            h_local(g, part).wait()
        u = groups + part

        def right_grad(j):
            k = span * part + j
            grads[pl.ds(pl.multiple_of(units[u][0] + j * blk, 16), blk)] = nn(p[k], cot[k]).astype(BF16)
        loop(span, right_grad)
        tick(u)
        if part < parts - 1:
            advance()
            if part < parts - 2:
                advance()
    while len(finished) < len(units):
        advance()
    loop(nl, lambda i: store_out(i).wait())
    for u in range(len(units)):
        for copy in result_copies(u):
            copy.wait()


def body(samples, gain, left_blocks, gate_blocks, right_blocks, cotangent, *, ndp, nmp):
    rows, width_local = samples.shape
    nl, blk = left_blocks.shape[0], left_blocks.shape[1]
    groups = nl // 8
    nk = nl * nmp
    units = [(g * 16 * blk, 16 * blk) for g in range(groups)]
    parts = 4
    span = nl // parts * blk
    units += [(2 * nl * blk + span * v, span) for v in range(parts)]
    flat = 3 * nl * blk
    dma = pltpu.SemaphoreType.DMA
    any_space = pl.BlockSpec(memory_space=pl.ANY)
    grad_input, *sums = pl.pallas_call(
        functools.partial(kernel, ndp, nmp, float(width_local * nmp), units, 2),
        out_shape=(
            jax.ShapeDtypeStruct((rows, width_local), BF16),
            *[jax.ShapeDtypeStruct((nl * blk, blk), BF16)] * 3,
        ),
        in_specs=[any_space, pl.BlockSpec(memory_space=pltpu.VMEM)] + [any_space] * 4,
        out_specs=(any_space,) * 4,
        scratch_shapes=[
            pltpu.VMEM((nl, rows, blk), BF16),
            pltpu.VMEM((nl, rows, blk), BF16),
            pltpu.VMEM((nl, blk, blk), BF16),
            pltpu.VMEM((nl, blk, blk), BF16),
            pltpu.VMEM((nl, blk, blk), BF16),
            pltpu.VMEM((nl, blk, rows), BF16),
            pltpu.VMEM((groups, nk, 16, rows), BF16),
            pltpu.VMEM((nl, blk, rows), BF16),
            pltpu.VMEM((groups, nk, 16, rows), BF16),
            pltpu.VMEM((nl, blk, rows), BF16),
            pltpu.VMEM((nl, blk, rows), BF16),
            pltpu.VMEM((nl, blk, rows), F32),
            pltpu.VMEM((nl, blk, rows), F32),
            pltpu.VMEM((nl, rows, blk), F32),
            pltpu.VMEM((flat, blk), BF16),
            pltpu.VMEM((flat, blk), BF16),
            pltpu.VMEM((flat, blk), BF16),
            pltpu.VMEM((rows, blk), F32),
            pltpu.VMEM((nmp, 8, rows), F32),
            pltpu.VMEM((nmp, 8, rows), F32),
            dma((2, nl)), dma((3,)), dma((nl,)), dma((1 + parts, groups)), dma((len(units), 2)),
            dma((nmp,)), dma((nmp,)),
            dma((nmp, groups)), dma((nmp, groups)),
            dma((nmp, groups, parts)), dma((nmp, groups, parts)),
            dma((nmp,)), dma((nmp,)),
            dma((len(units), ndp)), dma((len(units), ndp)),
            dma((len(units), ndp)), dma((len(units), ndp)),
        ],
        compiler_params=pltpu.CompilerParams(
            collective_id=0, has_side_effects=True, vmem_limit_bytes=60 * 1024 * 1024),
    )(samples, gain.reshape(nl, 1, blk), left_blocks, gate_blocks, right_blocks, cotangent)
    grad_left, grad_gate, grad_right = (v.reshape(nl, blk, blk).astype(F32) for v in sums)
    return grad_input, grad_left, grad_gate, grad_right


def solution(mesh):
    blocks = P("mp", None, None)
    return jax.shard_map(
        functools.partial(body, ndp=mesh.shape["dp"], nmp=mesh.shape["mp"]),
        mesh=mesh,
        in_specs=(P("dp", "mp"), P("mp"), blocks, blocks, blocks, P("dp", "mp")),
        out_specs=(P("dp", "mp"), blocks, blocks, blocks),
        check_vma=False,
    )
```
